256 devices in a mesh: cp: 32 (over y, x, core), hd: 8 (over z).
Axes of the slice: x: 4, y: 4, z: 8, core: 2. Of those that a mesh axis runs over, the one named last changes fastest.
Arguments:
- queries: bfloat16 [16384, 8192], P('cp', 'hd'), may hold values from -4.5 to 4.5
- keys: bfloat16 [16384, 1024], P(('cp', 'hd')), may hold values from -4.5 to 4.5
- values: bfloat16 [16384, 1024], P(('cp', 'hd')), may hold values from -6 to 6
- grads_out: bfloat16 [16384, 8192], P('cp', 'hd'), may hold values from -6 to 6
- doc_lengths: int32 [64], replicated, may hold values from 1 to 1536, 16384 in all
Outputs:
- attention_out: bfloat16 [16384, 8192], P('cp', 'hd')
- grad_queries: bfloat16 [16384, 8192], P('cp', 'hd')
- grad_keys: bfloat16 [16384, 1024], P(('cp', 'hd'))
- grad_values: bfloat16 [16384, 1024], P(('cp', 'hd'))
The draws below stay inside these ranges and needn't reach their ends.
Inputs may be any that keep to these rules, and one draw needn't show every extreme that they name: `doc_lengths`: the lengths of the 64 documents in order; they sum to 16384 and the largest is exactly 1536.
All inputs are finite; a program needn't handle non-finite values.
Results may differ from the reference program's by a relative error of at most 0.025.
Values may be sent and summed in bfloat16 or wider, within the bound.
A program may use at most 128 MiB of HBM per device.

```python
import math
import jax
import jax.numpy as jnp
import numpy as np
from jax import lax

QH = 64
KVH = 8
HD = 128
TOK_DEV = 512
REACH = 3
TOKENS = 16384
DOC_MOST = 1536
DOCS = 64
N_CP = 32


def draw_queries(key, part):
    key = jax.random.fold_in(key, 31)
    sample = jnp.clip(jax.random.normal(key, (TOKENS, QH * HD), jnp.float32), -4.5, 4.5)
    return sample.astype(jnp.bfloat16)


def draw_keys(key, part):
    key = jax.random.fold_in(key, 37)
    sample = jnp.clip(jax.random.normal(key, (TOKENS, KVH * HD), jnp.float32), -4.5, 4.5)
    return sample.astype(jnp.bfloat16)


def steps_of(rng, dims, cuts, low, top_value):
    def one(axis_at, blocks):
        steps = jax.random.uniform(jax.random.fold_in(jax.random.fold_in(rng, 6), axis_at), (blocks,), jnp.float32, low / len(cuts), top_value / len(cuts))
        return jnp.repeat(jnp.exp(steps), dims[axis_at] // blocks).reshape((-1,) + (1,) * (len(dims) - axis_at - 1))

    factor_of = one(*cuts[0])
    for cut in cuts[1:]:
        factor_of = factor_of * one(*cut)
    return factor_of


def profile(amount, total, bound, lean):
    loads = [(1 << 20) // math.isqrt(rank ** lean) + 1 for rank in range(2, amount + 1)]
    spare, holding = total - bound - (amount - 1), [1] * (amount - 1)
    while spare > 0:
        free = [i for i in range(amount - 1) if holding[i] < bound]
        mass, remaining = sum([loads[i] for i in free]), spare
        for i in free:
            extra = min(bound - holding[i], max(1, remaining * loads[i] // mass), spare)
            holding[i] = holding[i] + extra
            spare = spare - extra
    return np.array([bound] + holding)


def ragged(own_key, amount, total, reach, skew):
    if amount == 2:
        one = jax.random.randint(own_key, (), max(1, total - reach), min(reach, total - 1) + 1)
        return jnp.stack([one, total - one])
    tallies = jnp.asarray(profile(amount, total, reach, skew), jnp.int32)
    couples = (amount - 1) // 2
    source_of, sink = tallies[1:1 + 2 * couples:2], tallies[2:2 + 2 * couples:2]
    margin = jnp.minimum(source_of - 1, reach - sink)
    moved = jax.random.randint(jax.random.fold_in(own_key, 1), (couples,), 0, 1 << 20) % (margin + 1)
    tallies = tallies.at[1:1 + 2 * couples:2].set(source_of - moved).at[2:2 + 2 * couples:2].set(sink + moved)
    return tallies[jax.random.permutation(jax.random.fold_in(own_key, 2), amount)]


def normal_values(stream_key, shape, scale, most, shards=(), kind=jnp.bfloat16):
    factor_of = steps_of(stream_key, shape, shards, -0.22, 0.18) if shards else 1.0
    array = jax.random.normal(stream_key, shape, jnp.float32) * scale * factor_of
    return jnp.minimum(jnp.maximum(array, -most), most).astype(kind)


def setup_inputs(seed: int = 0) -> dict:
    key_list = jax.random.split(jax.random.key(seed), 6)
    queries = draw_queries(jax.random.fold_in(key_list[5], 71), 0)
    keys = draw_keys(jax.random.fold_in(key_list[5], 71), 0)
    values = normal_values(key_list[2], (TOKENS, KVH * HD), 1.0, 6.0, ((0, 256),))
    grads_out = normal_values(key_list[3], (TOKENS, QH * HD), 1.0, 6.0, ((0, 32), (1, 8)))
    doc_lengths = ragged(key_list[4], DOCS, TOKENS, DOC_MOST, 2).astype(jnp.int32)
    return {"queries": queries, "keys": keys, "values": values, "grads_out": grads_out, "doc_lengths": doc_lengths}


NEGATIVE = -1e+30

def doc_index(positions, starts):
    return lax.optimization_barrier(jnp.sum((starts[None, :] <= positions[:, None]).astype(jnp.int32), axis=1)) - 1

def round_trip(tensor):
    return lax.optimization_barrier(tensor.astype(jnp.bfloat16)).astype(jnp.float32)

def reference(queries, keys, values, grads_out, doc_lengths):
    group_size = QH // KVH
    window = (REACH + 1) * TOK_DEV
    score_scale = 1.0 / math.sqrt(HD)
    starts = (jnp.cumsum(doc_lengths) - doc_lengths).astype(jnp.int32)
    padding = jnp.zeros((REACH * TOK_DEV, KVH * HD), keys.dtype)
    keys_pad = jnp.concatenate([padding, keys], axis=0)
    values_pad = jnp.concatenate([padding, values], axis=0)

    def one_block(sums_carry, block_index):
        key_sums, value_sums = sums_carry
        first_row = (block_index * TOK_DEV).astype(jnp.int32)
        query_block = lax.dynamic_slice_in_dim(queries, first_row, TOK_DEV, 0).astype(jnp.float32).reshape(TOK_DEV, KVH, group_size, HD)
        grad_block = lax.dynamic_slice_in_dim(grads_out, first_row, TOK_DEV, 0).astype(jnp.float32).reshape(TOK_DEV, KVH, group_size, HD)
        key_window = lax.dynamic_slice_in_dim(keys_pad, first_row, window, 0).astype(jnp.float32).reshape(window, KVH, HD)
        value_window = lax.dynamic_slice_in_dim(values_pad, first_row, window, 0).astype(jnp.float32).reshape(window, KVH, HD)
        query_pos = first_row + jnp.arange(TOK_DEV, dtype=jnp.int32)
        key_pos = first_row - REACH * TOK_DEV + jnp.arange(window, dtype=jnp.int32)
        allowed = (doc_index(query_pos, starts)[:, None] == doc_index(key_pos, starts)[None, :]) & (key_pos[None, :] <= query_pos[:, None])
        scores = jnp.einsum('qagd,kad->agqk', query_block, key_window) * score_scale
        row_max = lax.optimization_barrier(jnp.max(jnp.where(allowed, scores, NEGATIVE), axis=-1))
        shifted = jnp.where(allowed, jnp.exp(scores - row_max[..., None]), 0.0)
        row_total = lax.optimization_barrier(jnp.sum(shifted, axis=-1))
        log_total = row_max + jnp.log(row_total)
        weights = round_trip(shifted)
        out_heads = jnp.einsum('agqk,kad->qagd', weights, value_window) / jnp.transpose(row_total, (2, 0, 1))[..., None]
        out_block = out_heads.astype(jnp.bfloat16)
        row_delta = jnp.transpose(lax.optimization_barrier(jnp.sum(grad_block * out_block.astype(jnp.float32), axis=-1)), (1, 2, 0))
        prob_tile = jnp.where(allowed, jnp.exp(scores - log_total[..., None]), 0.0)
        dprobs = jnp.einsum('qagd,kad->agqk', grad_block, value_window)
        dscores = round_trip(prob_tile * (dprobs - row_delta[..., None]) * score_scale)
        prob_rounded = round_trip(prob_tile)
        grad_query = jnp.einsum('agqk,kad->qagd', dscores, key_window).astype(jnp.bfloat16)
        grad_key = jnp.einsum('agqk,qagd->kad', dscores, query_block).reshape(window, KVH * HD)
        grad_value = jnp.einsum('agqk,qagd->kad', prob_rounded, grad_block).reshape(window, KVH * HD)
        key_sums = lax.dynamic_update_slice_in_dim(key_sums, lax.dynamic_slice_in_dim(key_sums, first_row, window, 0) + grad_key, first_row, 0)
        value_sums = lax.dynamic_update_slice_in_dim(value_sums, lax.dynamic_slice_in_dim(value_sums, first_row, window, 0) + grad_value, first_row, 0)
        return ((key_sums, value_sums), (out_block.reshape(TOK_DEV, QH * HD), grad_query.reshape(TOK_DEV, QH * HD)))
    zero_sums = jnp.zeros(((REACH + N_CP) * TOK_DEV, KVH * HD), jnp.float32)
    (key_sums, value_sums), (out_blocks, query_blocks) = lax.scan(one_block, (zero_sums, zero_sums), jnp.arange(N_CP, dtype=jnp.int32))
    attention_out = out_blocks.reshape(TOKENS, QH * HD)
    grad_queries = query_blocks.reshape(TOKENS, QH * HD)
    grad_keys = key_sums[REACH * TOK_DEV:].astype(jnp.bfloat16)
    grad_values = value_sums[REACH * TOK_DEV:].astype(jnp.bfloat16)
    return (attention_out, grad_queries, grad_keys, grad_values)
```

```python
import functools
import math

import jax
import jax.numpy as jnp
from jax import lax
from jax.experimental import pallas as pl
from jax.experimental.pallas import tpu as pltpu
from jax.sharding import PartitionSpec as P

HD = 128
REACH = 3
HALF = 256
ONES = 16
MASKED = -1e30
FLOOR = -5e29
MESH = pl.DeviceIdType.MESH
F32 = jnp.float32
BF16 = jnp.bfloat16


def dot(a, b):
    return jnp.dot(a, b, preferred_element_type=F32)


def key_range(distance, part, block):
    if distance == 0 and part == 0:
        return 0, HALF
    if distance == REACH and part == 1:
        return HALF, block
    return 0, block


def kernel(
    n_cp,
    n_hd,
    heads,
    block,
    doc_ref,
    k_ref,
    v_ref,
    q_ref,
    g_ref,
    out_ref,
    dq_ref,
    dk_ref,
    dv_ref,
    qs,
    gs,
    qt,
    gt,
    kv,
    kt,
    vt,
    first,
    weights,
    acc,
    top,
    total,
    delta,
    dqa,
    outb,
    dqb,
    part_sum,
    sent,
    came,
    final,
    load_sem,
    store_sem,
    local_sem,
    a_send,
    a_recv,
    x_send,
    x_recv,
    r_send,
    r_recv,
    f_send,
    f_recv,
):
    cp = lax.axis_index("cp")
    hd = lax.axis_index("hd")
    core = lax.rem(cp, 2)
    rows = block // n_hd
    scale = 1.0 / math.sqrt(HD)
    log_scale = scale * math.log2(math.e)

    def cp_at(step):
        return {"cp": lax.rem(cp + step + n_cp, n_cp)}

    def hd_at(step):
        return {"hd": lax.rem(hd + step, n_hd)}

    def columns(index):
        return pl.ds(pl.multiple_of(index * HD, HD), HD)

    def remote(src, dst, send_sem, recv_sem, device):
        return pltpu.make_async_remote_copy(
            src_ref=src,
            dst_ref=dst,
            send_sem=send_sem,
            recv_sem=recv_sem,
            device_id=device,
            device_id_type=MESH,
        )

    def load(which, h):
        source, target = ((q_ref, qs), (g_ref, gs))[which]
        return pltpu.make_async_copy(
            source.at[:, columns(h)], target.at[h], load_sem.at[which, h]
        )

    def store(which, h):
        source, target = ((outb, out_ref), (dqb, dq_ref))[which]
        return pltpu.make_async_copy(
            source.at[h], target.at[:, columns(h)], store_sem.at[which, h]
        )

    for which in range(2):
        for h in range(heads):
            load(which, h).start()
    barrier = pltpu.get_barrier_semaphore()
    for step in range(1, n_hd):
        pl.semaphore_signal(barrier, inc=1, device_id=hd_at(step), device_id_type=MESH)
    for step in (-2, -1, 1, 2):
        pl.semaphore_signal(barrier, inc=1, device_id=cp_at(step), device_id_type=MESH)
    pl.semaphore_wait(barrier, n_hd - 1 + 4)

    def exchange(which, step):
        source = (k_ref, v_ref)[which]
        peer = lax.rem(hd + step, n_hd)
        return remote(
            source.at[:, columns(peer)],
            kv.at[0, which, pl.ds(pl.multiple_of(hd * rows, rows), rows)],
            a_send.at[which, step],
            a_recv.at[which, step],
            {"hd": peer},
        )

    def exchange_own(which):
        source = (k_ref, v_ref)[which]
        return pltpu.make_async_copy(
            source.at[:, columns(hd)],
            kv.at[0, which, pl.ds(pl.multiple_of(hd * rows, rows), rows)],
            local_sem.at[which],
        )

    order = sorted(range(1, n_hd), key=lambda step: -min(step, n_hd - step))
    for which in range(2):
        for step in order:
            exchange(which, step).start()
        exchange_own(which).start()

    def ahead(which):
        return remote(
            kv.at[0, which], kv.at[2, which], x_send.at[0, which], x_recv.at[2, which], cp_at(2)
        )

    def beside_even(which):
        return remote(
            kv.at[0, which], kv.at[1, which], x_send.at[1, which], x_recv.at[1, which], cp_at(1)
        )

    def beside_odd(which):
        return remote(
            kv.at[2, which], kv.at[1, which], x_send.at[1, which], x_recv.at[1, which], cp_at(-1)
        )

    def onward(which):
        return remote(
            kv.at[2, which], kv.at[3, which], x_send.at[2, which], x_recv.at[3, which], cp_at(1)
        )

    position = cp * block + lax.broadcasted_iota(jnp.int32, (8, block), 1)

    def next_doc(i, carry):
        begin, start = carry
        begin = begin + doc_ref[i]
        return begin, jnp.where(position >= begin, begin, start)

    _, start = lax.fori_loop(
        0, doc_ref.shape[0], next_doc, (jnp.int32(0), jnp.zeros((8, block), jnp.int32))
    )
    first[...] = start - cp * block

    for which in range(2):
        for h in range(heads):
            load(which, h).wait()

    def turn_queries(h, _):
        qt[h] = qs[h].T
        gt[h] = gs[h].T
        return 0

    lax.fori_loop(0, heads, turn_queries, 0)
    for d in range(REACH + 1):
        vt[d, HD:, :] = jnp.ones((ONES, block), BF16)

    for which in range(2):
        for step in order:
            exchange(which, step).wait_recv()
        exchange_own(which).wait()
        ahead(which).start()

        @pl.when(core == 0)
        def _(which=which):
            beside_even(which).start()

    def turn_keys(d):
        kt[d] = kv[d, 0].T
        vt[d, :HD, :] = kv[d, 1].T

    def forward(d, h):
        for part in range(2):
            cols = slice(part * HALF, (part + 1) * HALF)
            low, high = key_range(d, part, block)
            scores = dot(kv[d, 0, low:high, :], qt[h, :, cols]) * log_scale
            shape = (high - low, HALF)
            key_pos = lax.broadcasted_iota(jnp.int32, shape, 0) + (low - d * block)
            allowed = key_pos >= first[0:1, cols]
            if d == 0:
                query_pos = lax.broadcasted_iota(jnp.int32, shape, 1) + part * HALF
                allowed = allowed & (key_pos <= query_pos)
            scores = jnp.where(allowed, scores, MASKED)
            peak = jnp.maximum(jnp.max(scores, axis=0, keepdims=True), FLOOR)
            tile = jnp.exp2(scores - peak).astype(BF16)
            weights[d, h, low:high, cols] = tile
            value = dot(vt[d, :, low:high], tile)
            acc[d, h, :, cols] = value[:HD]
            total[d, h, :, cols] = value[HD : HD + 8]
            top[d, h, :, cols] = jnp.broadcast_to(peak, (8, HALF))

    def finish(h):
        peaks = [top[d, h] for d in range(REACH + 1)]
        peak = functools.reduce(jnp.maximum, peaks)
        factors = [jnp.exp2(one - peak) for one in peaks]
        sums = functools.reduce(
            jnp.add, [factors[d] * total[d, h] for d in range(REACH + 1)]
        )
        inverse = 1.0 / sums
        value = None
        for d in range(REACH + 1):
            factor = factors[d] * inverse
            top[d, h] = factor
            term = acc[d, h] * factor[0:1]
            value = term if value is None else value + term
        rounded = value.astype(BF16)
        delta[h] = jnp.broadcast_to(
            jnp.sum(gt[h].astype(F32) * rounded.astype(F32), axis=0, keepdims=True), (8, block)
        )
        outb[h] = rounded.T
        store(0, h).start()

    def backward(d, h, first_term):
        for part in range(2):
            cols = slice(part * HALF, (part + 1) * HALF)
            low, high = key_range(d, part, block)
            prob = weights[d, h, low:high, cols].astype(F32) * top[d, h, 0:1, cols]
            dprob = dot(kv[d, 1, low:high, :], gt[h, :, cols])
            dscore = (prob * (dprob - delta[h, 0:1, cols])).astype(BF16)
            term = dot(kt[d, :, low:high], dscore)
            if first_term:
                dqa[h, :, cols] = term
            else:
                dqa[h, :, cols] += term
            part_sum[0, low:high, :] += dot(dscore, qs[h, cols, :])
            part_sum[1, low:high, :] += dot(prob.astype(BF16), gs[h, cols, :])

    def forward_all(d, last):
        turn_keys(d)

        def one(h, _):
            forward(d, h)
            if last:
                finish(h)
            return 0

        lax.fori_loop(0, heads, one, 0)

    forward_all(0, False)
    for which in range(2):
        ahead(which).wait_recv()
        onward(which).start()

        @pl.when(core == 1)
        def _(which=which):
            beside_odd(which).start()

    forward_all(2, False)
    for which in range(2):
        beside_even(which).wait_recv()
    forward_all(1, False)
    for which in range(2):
        onward(which).wait_recv()
    forward_all(3, True)

    def grads_back(which):
        return remote(
            sent.at[0, which], came.at[0, which], r_send.at[0, which], r_recv.at[0, which], cp_at(-1)
        )

    def grads_beside(which, step):
        return remote(
            sent.at[1, which],
            came.at[1, which],
            r_send.at[1, which],
            r_recv.at[1, which],
            cp_at(step),
        )

    def grads_chip(which):
        return remote(
            sent.at[2, which], came.at[2, which], r_send.at[2, which], r_recv.at[2, which], cp_at(-2)
        )

    def backward_all(d, first_term, last):
        part_sum[...] = jnp.zeros_like(part_sum)

        def one(h, _):
            backward(d, h, first_term)
            if last:
                dqb[h] = (dqa[h] * scale).astype(BF16).T
                store(1, h).start()
            return 0

        lax.fori_loop(0, heads, one, 0)

    factors = (scale, 1.0)
    backward_all(3, True, False)
    for which in range(2):
        sent[0, which] = (part_sum[which] * factors[which]).astype(BF16)
        grads_back(which).start()
    backward_all(1, False, False)
    for which in range(2):
        sent[1, which] = (part_sum[which] * factors[which]).astype(BF16)

        @pl.when(core == 0)
        def _(which=which):
            grads_beside(which, 1).start()

        @pl.when(core == 1)
        def _(which=which):
            grads_beside(which, -1).start()

    backward_all(2, False, False)
    for which in range(2):
        grads_back(which).wait_recv()
        chip_sum = part_sum[which] * factors[which] + came[0, which].astype(F32)

        @pl.when(core == 0)
        def _(which=which, chip_sum=chip_sum):
            sent[2, which] = chip_sum.astype(BF16)

        @pl.when(core == 1)
        def _(which=which, chip_sum=chip_sum):
            grads_beside(which, -1).wait_recv()
            sent[2, which] = (chip_sum + came[1, which].astype(F32)).astype(BF16)

        grads_chip(which).start()
    backward_all(0, False, True)

    def give(which, step):
        target = (dk_ref, dv_ref)[which]
        peer = lax.rem(hd + step, n_hd)
        return remote(
            final.at[which, pl.ds(pl.multiple_of(peer * rows, rows), rows)],
            target.at[:, columns(hd)],
            f_send.at[which, step],
            f_recv.at[which, step],
            {"hd": peer},
        )

    def give_own(which):
        target = (dk_ref, dv_ref)[which]
        return pltpu.make_async_copy(
            final.at[which, pl.ds(pl.multiple_of(hd * rows, rows), rows)],
            target.at[:, columns(hd)],
            local_sem.at[which],
        )

    for which in range(2):
        grads_chip(which).wait_recv()
        whole = part_sum[which] * factors[which] + came[2, which].astype(F32)

        @pl.when(core == 0)
        def _(which=which, whole=whole):
            grads_beside(which, 1).wait_recv()
            final[which] = (whole + came[1, which].astype(F32)).astype(BF16)

        @pl.when(core == 1)
        def _(which=which, whole=whole):
            final[which] = whole.astype(BF16)

        for step in order:
            give(which, step).start()
        give_own(which).start()

    for which in range(2):
        for step in order:
            give(which, step).wait_recv()
        give_own(which).wait()
    for which in range(2):
        for step in order:
            exchange(which, step).wait_send()
            give(which, step).wait_send()
        ahead(which).wait_send()
        beside_even(which).wait_send()
        onward(which).wait_send()
        grads_back(which).wait_send()
        grads_beside(which, 1).wait_send()
        grads_chip(which).wait_send()
        for h in range(heads):
            store(which, h).wait()


def on_device(n_cp, n_hd, queries, keys, values, grads_out, doc_lengths):
    block, width = queries.shape
    heads = width // HD
    blocks = REACH + 1
    vmem = pltpu.VMEM
    dma = pltpu.SemaphoreType.DMA
    anywhere = pl.BlockSpec(memory_space=pl.ANY)
    products = 6 * heads * 14 * HALF * HALF * HD * 2
    return pl.pallas_call(
        functools.partial(kernel, n_cp, n_hd, heads, block),
        out_shape=(
            jax.ShapeDtypeStruct(queries.shape, BF16),
            jax.ShapeDtypeStruct(queries.shape, BF16),
            jax.ShapeDtypeStruct(keys.shape, BF16),
            jax.ShapeDtypeStruct(values.shape, BF16),
        ),
        in_specs=[pl.BlockSpec(memory_space=pltpu.SMEM)] + [anywhere] * 4,
        out_specs=(anywhere,) * 4,
        scratch_shapes=[
            vmem((heads, block, HD), BF16),
            vmem((heads, block, HD), BF16),
            vmem((heads, HD, block), BF16),
            vmem((heads, HD, block), BF16),
            vmem((blocks, 2, block, HD), BF16),
            vmem((blocks, HD, block), BF16),
            vmem((blocks, HD + ONES, block), BF16),
            vmem((8, block), jnp.int32),
            vmem((blocks, heads, block, block), BF16),
            vmem((blocks, heads, HD, block), F32),
            vmem((blocks, heads, 8, block), F32),
            vmem((blocks, heads, 8, block), F32),
            vmem((heads, 8, block), F32),
            vmem((heads, HD, block), F32),
            vmem((heads, block, HD), BF16),
            vmem((heads, block, HD), BF16),
            vmem((2, block, HD), F32),
            vmem((3, 2, block, HD), BF16),
            vmem((3, 2, block, HD), BF16),
            vmem((2, block, HD), BF16),
            dma((2, heads)),
            dma((2, heads)),
            dma((2,)),
            dma((2, n_hd)),
            dma((2, n_hd)),
            dma((3, 2)),
            dma((4, 2)),
            dma((3, 2)),
            dma((3, 2)),
            dma((2, n_hd)),
            dma((2, n_hd)),
        ],
        compiler_params=pltpu.CompilerParams(
            collective_id=0, has_side_effects=True, vmem_limit_bytes=56 * 2**20
        ),
        cost_estimate=pl.CostEstimate(
            flops=products, bytes_accessed=8 * 2**20, transcendentals=products // (12 * HD)
        ),
    )(doc_lengths, keys, values, queries, grads_out)


def solution(mesh):
    in_specs = (P("cp", "hd"), P(("cp", "hd"), None), P(("cp", "hd"), None), P("cp", "hd"), P())
    out_specs = (P("cp", "hd"), P("cp", "hd"), P(("cp", "hd"), None), P(("cp", "hd"), None))
    return jax.shard_map(
        functools.partial(on_device, mesh.shape["cp"], mesh.shape["hd"]),
        mesh=mesh,
        in_specs=in_specs,
        out_specs=out_specs,
        check_vma=False,
    )
```

```python
import functools
import math

import jax
import jax.numpy as jnp
from jax import lax
from jax.experimental import pallas as pl
from jax.experimental.pallas import tpu as pltpu
from jax.sharding import PartitionSpec as P

HD = 128
REACH = 3
HALF = 256
ONES = 16
MASKED = -1e30
FLOOR = -5e29
CEILING = 1e30
MESH = pl.DeviceIdType.MESH
F32 = jnp.float32
BF16 = jnp.bfloat16


def dot(a, b):
    return jnp.dot(a, b, preferred_element_type=F32)


def key_range(distance, part, block):
    if distance == 0 and part == 0:
        return 0, HALF
    if distance == REACH and part == 1:
        return HALF, block
    return 0, block


def kernel(
    n_cp,
    n_hd,
    heads,
    block,
    doc_ref,
    k_ref,
    v_ref,
    q_ref,
    g_ref,
    out_ref,
    dq_ref,
    dk_ref,
    dv_ref,
    qs,
    gs,
    qt,
    gt,
    kv,
    ks,
    kt,
    vt,
    first,
    begin,
    bias,
    weights,
    acc,
    top,
    total,
    delta,
    dqa,
    outb,
    dqb,
    part_sum,
    sent,
    came,
    final,
    load_sem,
    store_sem,
    local_sem,
    a_send,
    a_recv,
    x_send,
    x_recv,
    r_send,
    r_recv,
    f_send,
    f_recv,
):
    cp = lax.axis_index("cp")
    hd = lax.axis_index("hd")
    core = lax.rem(cp, 2)
    rows = block // n_hd
    scale = 1.0 / math.sqrt(HD)
    log_scale = scale * math.log2(math.e)

    def cp_at(step):
        return {"cp": lax.rem(cp + step + n_cp, n_cp)}

    def hd_at(step):
        return {"hd": lax.rem(hd + step, n_hd)}

    def columns(index):
        return pl.ds(pl.multiple_of(index * HD, HD), HD)

    def remote(src, dst, send_sem, recv_sem, device):
        return pltpu.make_async_remote_copy(
            src_ref=src,
            dst_ref=dst,
            send_sem=send_sem,
            recv_sem=recv_sem,
            device_id=device,
            device_id_type=MESH,
        )

    def load(which, h):
        source, target = ((q_ref, qs), (g_ref, gs))[which]
        return pltpu.make_async_copy(
            source.at[:, columns(h)], target.at[h], load_sem.at[which, h]
        )

    def store(which, h):
        source, target = ((outb, out_ref), (dqb, dq_ref))[which]
        return pltpu.make_async_copy(
            source.at[h], target.at[:, columns(h)], store_sem.at[which, h]
        )

    for which in range(2):
        for h in range(heads):
            load(which, h).start()
    barrier = pltpu.get_barrier_semaphore()
    for step in range(1, n_hd):
        pl.semaphore_signal(barrier, inc=1, device_id=hd_at(step), device_id_type=MESH)
    for step in (-2, -1, 1, 2):
        pl.semaphore_signal(barrier, inc=1, device_id=cp_at(step), device_id_type=MESH)
    pl.semaphore_wait(barrier, n_hd - 1 + 4)

    def exchange(which, step):
        source = (k_ref, v_ref)[which]
        peer = lax.rem(hd + step, n_hd)
        return remote(
            source.at[:, columns(peer)],
            kv.at[0, which, pl.ds(pl.multiple_of(hd * rows, rows), rows)],
            a_send.at[which, step],
            a_recv.at[which, step],
            {"hd": peer},
        )

    def exchange_own(which):
        source = (k_ref, v_ref)[which]
        return pltpu.make_async_copy(
            source.at[:, columns(hd)],
            kv.at[0, which, pl.ds(pl.multiple_of(hd * rows, rows), rows)],
            local_sem.at[which],
        )

    order = sorted(range(1, n_hd), key=lambda step: -min(step, n_hd - step))
    for which in range(2):
        for step in order:
            exchange(which, step).start()
        exchange_own(which).start()

    def ahead(which):
        return remote(
            kv.at[0, which], kv.at[2, which], x_send.at[0, which], x_recv.at[2, which], cp_at(2)
        )

    def beside_even(which):
        return remote(
            kv.at[0, which], kv.at[1, which], x_send.at[1, which], x_recv.at[1, which], cp_at(1)
        )

    def beside_odd(which):
        return remote(
            kv.at[2, which], kv.at[1, which], x_send.at[1, which], x_recv.at[1, which], cp_at(-1)
        )

    def onward(which):
        return remote(
            kv.at[2, which], kv.at[3, which], x_send.at[2, which], x_recv.at[3, which], cp_at(1)
        )

    position = cp * block + lax.broadcasted_iota(jnp.int32, (8, block), 1)
    corner = jnp.full((ONES, block), cp * block, jnp.int32)

    def next_doc(i, carry):
        edge, start, start_first = carry
        edge = edge + doc_ref[i]
        return (
            edge,
            jnp.where(position >= edge, edge, start),
            jnp.where(corner >= edge, edge, start_first),
        )

    _, start, start_first = lax.fori_loop(
        0,
        doc_ref.shape[0],
        next_doc,
        (jnp.int32(0), jnp.zeros((8, block), jnp.int32), jnp.zeros((ONES, block), jnp.int32)),
    )
    first[...] = start - cp * block
    begin[...] = start_first - cp * block

    def mask_rows(i, _):
        rows_at = pl.ds(pl.multiple_of(i * 64, 64), 64)
        key_pos = lax.broadcasted_iota(jnp.int32, (64, block), 0) + i * 64
        query_pos = lax.broadcasted_iota(jnp.int32, (64, block), 1)
        allowed = (key_pos >= first[0:1, :]) & (key_pos <= query_pos)
        bias[rows_at, :] = jnp.where(allowed, 0.0, MASKED)
        return 0

    lax.fori_loop(0, block // 64, mask_rows, 0)

    for which in range(2):
        for h in range(heads):
            load(which, h).wait()

    def turn_queries(h, _):
        scaled = qs[h].astype(F32).T * log_scale
        high = scaled.astype(BF16)
        qt[h, :HD, :] = high
        qt[h, HD:, :] = (scaled - high.astype(F32)).astype(BF16)
        gt[h] = gs[h].T
        return 0

    lax.fori_loop(0, heads, turn_queries, 0)

    for which in range(2):
        for step in order:
            exchange(which, step).wait_recv()
        exchange_own(which).wait()
        ahead(which).start()

        @pl.when(core == 0)
        def _(which=which):
            beside_even(which).start()

    def key_kept(d):
        key_pos = lax.broadcasted_iota(jnp.int32, (block, HD), 0) - d * block
        return key_pos >= begin[0:1, :HD]

    def turn_keys(d):
        keys, values = kv[d, 0], kv[d, 1]
        if d == 0:
            ks[d] = keys
            kt[d] = keys.T
            vt[d, :HD, :] = values.T
            vt[d, HD:, :] = jnp.ones((ONES, block), BF16)
        else:
            kept = key_kept(d)
            wide = keys.astype(F32)
            ks[d] = jnp.where(kept, wide, wide[block - 1 :, :]).astype(BF16)
            kt[d] = jnp.where(kept, wide, 0.0).astype(BF16).T
            vt[d, :HD, :] = jnp.where(kept, values.astype(F32), 0.0).astype(BF16).T
            key_pos = lax.broadcasted_iota(jnp.int32, (ONES, block), 1) - d * block
            vt[d, HD:, :] = jnp.where(key_pos >= begin[...], 1.0, 0.0).astype(BF16)

    items = [(h, part) for h in range(heads) for part in range(2)]

    def cols_of(part):
        return slice(part * HALF, (part + 1) * HALF)

    def forward_all(d, last):
        turn_keys(d)

        def scores_of(h, part):
            low, high = key_range(d, part, block)
            keys = ks[d, low:high, :]
            return dot(jnp.concatenate([keys, keys], axis=1), qt[h, :, cols_of(part)])

        def softmax(h, part, scores):
            cols = cols_of(part)
            low, high = key_range(d, part, block)
            if d == 0:
                scores = scores + bias[low:high, cols]
                peak = jnp.max(scores, axis=0, keepdims=True)
                kept_peak = peak
            else:
                reached = first[0:1, cols] < (1 - d) * block
                peak = jnp.max(scores, axis=0, keepdims=True)
                kept_peak = jnp.where(reached, peak, FLOOR)
                peak = jnp.where(reached, peak, CEILING)
            tile = jnp.exp2(scores - peak).astype(BF16)
            weights[d, h, low:high, cols] = tile
            top[d, h, :, cols] = jnp.broadcast_to(kept_peak, (8, HALF))
            return tile

        def weighted(h, part, tile):
            cols = cols_of(part)
            low, high = key_range(d, part, block)
            value = dot(vt[d, :, low:high], tile)
            acc[d, h, :, cols] = value[:HD]
            total[d, h, :, cols] = value[HD : HD + 8]
            if last and part == 1:
                finish(h)

        ready = [scores_of(*item) for item in items[:2]]
        late = None
        for i, item in enumerate(items):
            if i + 2 < len(items):
                ready.append(scores_of(*items[i + 2]))
            tile = softmax(*item, ready.pop(0))
            if late is not None:
                weighted(*late)
            late = (*item, tile)
        weighted(*late)

    def finish(h):
        peaks = [top[d, h] for d in range(REACH + 1)]
        peak = functools.reduce(jnp.maximum, peaks)
        factors = [jnp.exp2(one - peak) for one in peaks]
        sums = functools.reduce(
            jnp.add, [factors[d] * total[d, h] for d in range(REACH + 1)]
        )
        inverse = 1.0 / sums
        value = None
        for d in range(REACH + 1):
            factor = factors[d] * inverse
            top[d, h] = factor
            term = acc[d, h] * factor[0:1]
            value = term if value is None else value + term
        rounded = value.astype(BF16)
        delta[h] = jnp.broadcast_to(
            jnp.sum(gt[h].astype(F32) * rounded.astype(F32), axis=0, keepdims=True), (8, block)
        )
        outb[h] = rounded.T
        store(0, h).start()

    def backward_all(d, first_term, last):
        part_sum[...] = jnp.zeros_like(part_sum)

        def dprob_of(h, part):
            low, high = key_range(d, part, block)
            return dot(kv[d, 1, low:high, :], gt[h, :, cols_of(part)])

        def products(h, part, prob, dscore):
            cols = cols_of(part)
            low, high = key_range(d, part, block)
            term = dot(kt[d, :, low:high], dscore)
            if first_term:
                dqa[h, :, cols] = term
            else:
                dqa[h, :, cols] += term
            part_sum[0, low:high, :] += dot(dscore, qs[h, cols, :])
            part_sum[1, low:high, :] += dot(prob, gs[h, cols, :])
            if last and part == 1:
                dqb[h] = (dqa[h] * scale).astype(BF16).T
                store(1, h).start()

        ready = [dprob_of(*item) for item in items[:2]]
        late = None
        for i, (h, part) in enumerate(items):
            if i + 2 < len(items):
                ready.append(dprob_of(*items[i + 2]))
            cols = cols_of(part)
            low, high = key_range(d, part, block)
            prob = weights[d, h, low:high, cols].astype(F32) * top[d, h, 0:1, cols]
            dscore = (prob * (ready.pop(0) - delta[h, 0:1, cols])).astype(BF16)
            if late is not None:
                products(*late)
            late = (h, part, prob.astype(BF16), dscore)
        products(*late)

    def block_grads(d, which):
        grads = part_sum[which] * (scale, 1.0)[which]
        return grads if d == 0 else jnp.where(key_kept(d), grads, 0.0)

    forward_all(0, False)
    for which in range(2):
        ahead(which).wait_recv()
        onward(which).start()

        @pl.when(core == 1)
        def _(which=which):
            beside_odd(which).start()

    forward_all(2, False)
    for which in range(2):
        beside_even(which).wait_recv()
    forward_all(1, False)
    for which in range(2):
        onward(which).wait_recv()
    forward_all(3, True)

    def grads_back(which):
        return remote(
            sent.at[0, which], came.at[0, which], r_send.at[0, which], r_recv.at[0, which], cp_at(-1)
        )

    def grads_beside(which, step):
        return remote(
            sent.at[1, which],
            came.at[1, which],
            r_send.at[1, which],
            r_recv.at[1, which],
            cp_at(step),
        )

    def grads_chip(which):
        return remote(
            sent.at[2, which], came.at[2, which], r_send.at[2, which], r_recv.at[2, which], cp_at(-2)
        )

    backward_all(3, True, False)
    for which in range(2):
        sent[0, which] = block_grads(3, which).astype(BF16)
        grads_back(which).start()
    backward_all(1, False, False)
    for which in range(2):
        sent[1, which] = block_grads(1, which).astype(BF16)

        @pl.when(core == 0)
        def _(which=which):
            grads_beside(which, 1).start()

        @pl.when(core == 1)
        def _(which=which):
            grads_beside(which, -1).start()

    backward_all(2, False, False)
    for which in range(2):
        grads_back(which).wait_recv()
        chip_sum = block_grads(2, which) + came[0, which].astype(F32)

        @pl.when(core == 0)
        def _(which=which, chip_sum=chip_sum):
            sent[2, which] = chip_sum.astype(BF16)

        @pl.when(core == 1)
        def _(which=which, chip_sum=chip_sum):
            grads_beside(which, -1).wait_recv()
            sent[2, which] = (chip_sum + came[1, which].astype(F32)).astype(BF16)

        grads_chip(which).start()
    backward_all(0, False, True)

    def give(which, step):
        target = (dk_ref, dv_ref)[which]
        peer = lax.rem(hd + step, n_hd)
        return remote(
            final.at[which, pl.ds(pl.multiple_of(peer * rows, rows), rows)],
            target.at[:, columns(hd)],
            f_send.at[which, step],
            f_recv.at[which, step],
            {"hd": peer},
        )

    def give_own(which):
        target = (dk_ref, dv_ref)[which]
        return pltpu.make_async_copy(
            final.at[which, pl.ds(pl.multiple_of(hd * rows, rows), rows)],
            target.at[:, columns(hd)],
            local_sem.at[which],
        )

    for which in range(2):
        grads_chip(which).wait_recv()
        whole = block_grads(0, which) + came[2, which].astype(F32)

        @pl.when(core == 0)
        def _(which=which, whole=whole):
            grads_beside(which, 1).wait_recv()
            final[which] = (whole + came[1, which].astype(F32)).astype(BF16)

        @pl.when(core == 1)
        def _(which=which, whole=whole):
            final[which] = whole.astype(BF16)

        for step in order:
            give(which, step).start()
        give_own(which).start()

    for which in range(2):
        for step in order:
            give(which, step).wait_recv()
        give_own(which).wait()
    for which in range(2):
        for step in order:
            exchange(which, step).wait_send()
            give(which, step).wait_send()
        ahead(which).wait_send()
        beside_even(which).wait_send()
        onward(which).wait_send()
        grads_back(which).wait_send()
        grads_beside(which, 1).wait_send()
        grads_chip(which).wait_send()
        for h in range(heads):
            store(which, h).wait()


def hand_over(*refs):
    count = len(refs) // 2
    sem = refs[-1]
    copies = []
    for i in range(count):
        source, target = refs[i], refs[count + i]
        parts = 4 if i < 2 else 1
        rows = source.shape[0] // parts
        for j in range(parts):
            at = slice(j * rows, (j + 1) * rows)
            copies.append(
                pltpu.make_async_copy(source.at[at], target.at[at], sem.at[len(copies)])
            )
    for copy in copies:
        copy.start()
    for copy in copies:
        copy.wait()


def on_device(n_cp, n_hd, queries, keys, values, grads_out, doc_lengths):
    block, width = queries.shape
    heads = width // HD
    blocks = REACH + 1
    vmem = pltpu.VMEM
    dma = pltpu.SemaphoreType.DMA
    anywhere = pl.BlockSpec(memory_space=pl.ANY)
    products = 6 * heads * 14 * HALF * HALF * HD * 2
    results = pl.pallas_call(
        functools.partial(kernel, n_cp, n_hd, heads, block),
        out_shape=(
            jax.ShapeDtypeStruct(queries.shape, BF16),
            jax.ShapeDtypeStruct(queries.shape, BF16),
            jax.ShapeDtypeStruct(keys.shape, BF16),
            jax.ShapeDtypeStruct(values.shape, BF16),
        ),
        in_specs=[pl.BlockSpec(memory_space=pltpu.SMEM)] + [anywhere] * 4,
        out_specs=(anywhere,) * 4,
        scratch_shapes=[
            vmem((heads, block, HD), BF16),
            vmem((heads, block, HD), BF16),
            vmem((heads, 2 * HD, block), BF16),
            vmem((heads, HD, block), BF16),
            vmem((blocks, 2, block, HD), BF16),
            vmem((blocks, block, HD), BF16),
            vmem((blocks, HD, block), BF16),
            vmem((blocks, HD + ONES, block), BF16),
            vmem((8, block), jnp.int32),
            vmem((ONES, block), jnp.int32),
            vmem((block, block), F32),
            vmem((blocks, heads, block, block), BF16),
            vmem((blocks, heads, HD, block), F32),
            vmem((blocks, heads, 8, block), F32),
            vmem((blocks, heads, 8, block), F32),
            vmem((heads, 8, block), F32),
            vmem((heads, HD, block), F32),
            vmem((heads, block, HD), BF16),
            vmem((heads, block, HD), BF16),
            vmem((2, block, HD), F32),
            vmem((3, 2, block, HD), BF16),
            vmem((3, 2, block, HD), BF16),
            vmem((2, block, HD), BF16),
            dma((2, heads)),
            dma((2, heads)),
            dma((2,)),
            dma((2, n_hd)),
            dma((2, n_hd)),
            dma((3, 2)),
            dma((4, 2)),
            dma((3, 2)),
            dma((3, 2)),
            dma((2, n_hd)),
            dma((2, n_hd)),
        ],
        compiler_params=pltpu.CompilerParams(
            collective_id=0, has_side_effects=True, vmem_limit_bytes=56 * 2**20
        ),
        cost_estimate=pl.CostEstimate(
            flops=products, bytes_accessed=8 * 2**20, transcendentals=products // (12 * HD)
        ),
    )(doc_lengths, keys, values, queries, grads_out)

    return pl.pallas_call(
        hand_over,
        out_shape=tuple(jax.ShapeDtypeStruct(one.shape, one.dtype) for one in results),
        in_specs=[anywhere] * 4,
        out_specs=(anywhere,) * 4,
        scratch_shapes=[dma((10,))],
        compiler_params=pltpu.CompilerParams(vmem_limit_bytes=56 * 2**20),
    )(*results)


def solution(mesh):
    in_specs = (P("cp", "hd"), P(("cp", "hd"), None), P(("cp", "hd"), None), P("cp", "hd"), P())
    out_specs = (P("cp", "hd"), P("cp", "hd"), P(("cp", "hd"), None), P(("cp", "hd"), None))
    return jax.shard_map(
        functools.partial(on_device, mesh.shape["cp"], mesh.shape["hd"]),
        mesh=mesh,
        in_specs=in_specs,
        out_specs=out_specs,
        check_vma=False,
    )
```

```python
import functools
import math

import jax
import jax.numpy as jnp
from jax import lax
from jax.experimental import pallas as pl
from jax.experimental.pallas import tpu as pltpu
from jax.sharding import PartitionSpec as P

HD = 128
REACH = 3
HALF = 256
ONES = 16
MASKED = -1e30
FLOOR = -5e29
CEILING = 1e30
MESH = pl.DeviceIdType.MESH
F32 = jnp.float32
BF16 = jnp.bfloat16


def dot(a, b):
    return jnp.dot(a, b, preferred_element_type=F32)


def key_range(distance, part, block):
    if distance == 0 and part == 0:
        return 0, HALF
    if distance == REACH and part == 1:
        return HALF, block
    return 0, block


def kernel(
    n_cp,
    n_hd,
    heads,
    block,
    doc_ref,
    k_ref,
    v_ref,
    q_ref,
    g_ref,
    out_ref,
    dq_ref,
    dk_ref,
    dv_ref,
    qs,
    gs,
    qt,
    gt,
    kv,
    ks,
    kt,
    vt,
    first,
    begin,
    bias,
    weights,
    acc,
    top,
    total,
    delta,
    outb,
    dqb,
    part_sum,
    held,
    sent,
    came,
    final,
    load_sem,
    store_sem,
    local_sem,
    a_send,
    a_recv,
    x_send,
    x_recv,
    r_send,
    r_recv,
    f_send,
    f_recv,
):
    cp = lax.axis_index("cp")
    hd = lax.axis_index("hd")
    core = lax.rem(cp, 2)
    rows = block // n_hd
    scale = 1.0 / math.sqrt(HD)
    log_scale = scale * math.log2(math.e)

    def cp_at(step):
        return {"cp": lax.rem(cp + step + n_cp, n_cp)}

    def hd_at(step):
        return {"hd": lax.rem(hd + step, n_hd)}

    def columns(index):
        return pl.ds(pl.multiple_of(index * HD, HD), HD)

    def remote(src, dst, send_sem, recv_sem, device):
        return pltpu.make_async_remote_copy(
            src_ref=src,
            dst_ref=dst,
            send_sem=send_sem,
            recv_sem=recv_sem,
            device_id=device,
            device_id_type=MESH,
        )

    def load(which, h):
        source, target = ((q_ref, qs), (g_ref, gs))[which]
        return pltpu.make_async_copy(
            source.at[:, columns(h)], target.at[h], load_sem.at[which, h]
        )

    def store(which, h):
        source, target = ((outb, out_ref), (dqb, dq_ref))[which]
        return pltpu.make_async_copy(
            source.at[h], target.at[:, columns(h)], store_sem.at[which, h]
        )

    for which in range(2):
        for h in range(heads):
            load(which, h).start()
    barrier = pltpu.get_barrier_semaphore()
    for step in range(1, n_hd):
        pl.semaphore_signal(barrier, inc=1, device_id=hd_at(step), device_id_type=MESH)
    for step in (-2, -1, 1, 2):
        pl.semaphore_signal(barrier, inc=1, device_id=cp_at(step), device_id_type=MESH)
    pl.semaphore_wait(barrier, n_hd - 1 + 4)

    def exchange(which, step):
        source = (k_ref, v_ref)[which]
        peer = lax.rem(hd + step, n_hd)
        return remote(
            source.at[:, columns(peer)],
            kv.at[0, which, pl.ds(pl.multiple_of(hd * rows, rows), rows)],
            a_send.at[which, step],
            a_recv.at[which, step],
            {"hd": peer},
        )

    def exchange_own(which):
        source = (k_ref, v_ref)[which]
        return pltpu.make_async_copy(
            source.at[:, columns(hd)],
            kv.at[0, which, pl.ds(pl.multiple_of(hd * rows, rows), rows)],
            local_sem.at[which],
        )

    order = sorted(range(1, n_hd), key=lambda step: -min(step, n_hd - step))
    for which in range(2):
        for step in order:
            exchange(which, step).start()
        exchange_own(which).start()

    def ahead(which, step=None):
        part = kv.at[0, which]
        target = kv.at[2, which]
        if step is not None:
            owner = lax.rem(hd - step + n_hd, n_hd)
            at = pl.ds(pl.multiple_of(owner * rows, rows), rows)
            part, target = part.at[at], target.at[at]
        return remote(part, target, x_send.at[0, which], x_recv.at[2, which], cp_at(2))

    def beside_even(which):
        return remote(
            kv.at[0, which], kv.at[1, which], x_send.at[1, which], x_recv.at[1, which], cp_at(1)
        )

    def beside_odd(which):
        return remote(
            kv.at[2, which], kv.at[1, which], x_send.at[1, which], x_recv.at[1, which], cp_at(-1)
        )

    def onward(which):
        return remote(
            kv.at[2, which], kv.at[3, which], x_send.at[2, which], x_recv.at[3, which], cp_at(1)
        )

    position = cp * block + lax.broadcasted_iota(jnp.int32, (8, block), 1)
    corner = jnp.full((ONES, block), cp * block, jnp.int32)

    def next_doc(i, carry):
        edge, start, start_first = carry
        edge = edge + doc_ref[i]
        return (
            edge,
            jnp.where(position >= edge, edge, start),
            jnp.where(corner >= edge, edge, start_first),
        )

    _, start, start_first = lax.fori_loop(
        0,
        doc_ref.shape[0],
        next_doc,
        (jnp.int32(0), jnp.zeros((8, block), jnp.int32), jnp.zeros((ONES, block), jnp.int32)),
    )
    first[...] = start - cp * block
    begin[...] = start_first - cp * block

    def mask_rows(i, _):
        rows_at = pl.ds(pl.multiple_of(i * 64, 64), 64)
        key_pos = lax.broadcasted_iota(jnp.int32, (64, block), 0) + i * 64
        query_pos = lax.broadcasted_iota(jnp.int32, (64, block), 1)
        allowed = (key_pos >= first[0:1, :]) & (key_pos <= query_pos)
        bias[rows_at, :] = jnp.where(allowed, 0.0, MASKED)
        return 0

    lax.fori_loop(0, block // 64, mask_rows, 0)

    for which in range(2):
        for h in range(heads):
            load(which, h).wait()

    def turn_queries(h, _):
        scaled = qs[h].astype(F32).T * log_scale
        high = scaled.astype(BF16)
        qt[h, :HD, :] = high
        qt[h, HD:, :] = (scaled - high.astype(F32)).astype(BF16)
        gt[h] = gs[h].T
        return 0

    lax.fori_loop(0, heads, turn_queries, 0)

    def arrive_own(which):
        exchange_own(which).wait()
        ahead(which, 0).start()
        for step in reversed(order):
            exchange(which, step).wait_recv()
            ahead(which, step).start()

        @pl.when(core == 0)
        def _():
            beside_even(which).start()

    def arrive_two_back(which):
        ahead(which).wait_recv()
        onward(which).start()

        @pl.when(core == 1)
        def _():
            beside_odd(which).start()

    def arrive_one_back(which):
        beside_even(which).wait_recv()

    def arrive_three_back(which):
        onward(which).wait_recv()

    def key_rows(d, low=0, high=block):
        begin_at = (REACH - d) * block + low
        if not isinstance(d, int):
            begin_at = pl.multiple_of(begin_at, HALF)
        return pl.ds(begin_at, high - low)

    def key_kept(d):
        key_pos = lax.broadcasted_iota(jnp.int32, (block, HD), 0) - d * block
        return key_pos >= begin[0:1, :HD]

    def turn_keys(d):
        keys = kv[d, 0]
        if d == 0:
            ks[d] = keys
            kt[:, key_rows(d)] = keys.T
        else:
            kept = key_kept(d)
            wide = keys.astype(F32)
            ks[d] = jnp.where(kept, wide, wide[block - 1 :, :]).astype(BF16)
            kt[:, key_rows(d)] = jnp.where(kept, wide, 0.0).astype(BF16).T

    def turn_values(d):
        values = kv[d, 1]
        if d == 0:
            vt[d, :HD, :] = values.T
            vt[d, HD:, :] = jnp.ones((ONES, block), BF16)
        else:
            vt[d, :HD, :] = jnp.where(key_kept(d), values.astype(F32), 0.0).astype(BF16).T
            key_pos = lax.broadcasted_iota(jnp.int32, (ONES, block), 1) - d * block
            vt[d, HD:, :] = jnp.where(key_pos >= begin[...], 1.0, 0.0).astype(BF16)

    items = [(h, part) for h in range(heads) for part in range(2)]

    def cols_of(part):
        return slice(part * HALF, (part + 1) * HALF)

    def forward_all(d, arrive, last, values_last=False):
        arrive(0)
        turn_keys(d)

        def scores_of(h, part):
            low, high = key_range(d, part, block)
            keys = ks[d, low:high, :]
            return dot(jnp.concatenate([keys, keys], axis=1), qt[h, :, cols_of(part)])

        def softmax(h, part, scores):
            cols = cols_of(part)
            low, high = key_range(d, part, block)
            if d == 0:
                scores = scores + bias[low:high, cols]
                peak = jnp.max(scores, axis=0, keepdims=True)
                kept_peak = peak
            else:
                reached = first[0:1, cols] < (1 - d) * block
                peak = jnp.max(scores, axis=0, keepdims=True)
                kept_peak = jnp.where(reached, peak, FLOOR)
                peak = jnp.where(reached, peak, CEILING)
            tile = jnp.exp2(scores - peak).astype(BF16)
            weights[h, key_rows(d, low, high), cols] = tile
            top[d, h, :, cols] = jnp.broadcast_to(kept_peak, (8, HALF))
            return tile

        def weighted(h, part, tile):
            cols = cols_of(part)
            low, high = key_range(d, part, block)
            value = dot(vt[d, :, low:high], tile)
            acc[d, h, :, cols] = value[:HD]
            total[d, h, :, cols] = value[HD : HD + 8]
            if last and part == 1:
                finish(h)

        ready = [scores_of(*item) for item in items[:2]]
        late = None
        for i, item in enumerate(items):
            if i + 2 < len(items):
                ready.append(scores_of(*items[i + 2]))
            tile = softmax(*item, ready.pop(0))
            if values_last:
                continue
            if late is None:
                arrive(1)
                turn_values(d)
            else:
                weighted(*late)
            late = (*item, tile)
        if values_last:
            arrive(1)
            turn_values(d)
            for h, part in items:
                low, high = key_range(d, part, block)
                weighted(h, part, weights[h, key_rows(d, low, high), cols_of(part)])
        else:
            weighted(*late)

    def finish(h):
        peaks = [top[d, h] for d in range(REACH + 1)]
        peak = functools.reduce(jnp.maximum, peaks)
        factors = [jnp.exp2(one - peak) for one in peaks]
        sums = functools.reduce(
            jnp.add, [factors[d] * total[d, h] for d in range(REACH + 1)]
        )
        inverse = 1.0 / sums
        value = None
        for d in range(REACH + 1):
            factor = factors[d] * inverse
            top[d, h] = factor
            term = acc[d, h] * factor[0:1]
            value = term if value is None else value + term
        rounded = value.astype(BF16)
        delta[h] = jnp.broadcast_to(
            jnp.sum(gt[h].astype(F32) * rounded.astype(F32), axis=0, keepdims=True), (8, block)
        )
        outb[h] = rounded.T
        store(0, h).start()

    def prob_of(d, like, h, part):
        cols = cols_of(part)
        low, high = key_range(like, part, block)
        return weights[h, key_rows(d, low, high), cols].astype(F32) * top[d, h, 0:1, cols]

    def add_values(d, like, h, part, prob):
        low, high = key_range(like, part, block)
        part_sum[1, low:high, :] += dot(prob, gs[h, cols_of(part), :])

    def backward_all(d, like, halfway=None, values_first=False):
        part_sum[...] = jnp.zeros_like(part_sum)
        if values_first:
            for h, part in items:
                add_values(d, like, h, part, prob_of(d, like, h, part).astype(BF16))

        def dprob_of(h, part):
            low, high = key_range(like, part, block)
            return dot(kv[d, 1, low:high, :], gt[h, :, cols_of(part)])

        def products(h, part, prob, dscore):
            low, high = key_range(like, part, block)
            part_sum[0, low:high, :] += dot(dscore, qs[h, cols_of(part), :])
            if not values_first:
                add_values(d, like, h, part, prob)

        ready = [dprob_of(*item) for item in items[:2]]
        late = None
        for i, (h, part) in enumerate(items):
            if halfway is not None and i == heads:
                halfway()
            if i + 2 < len(items):
                ready.append(dprob_of(*items[i + 2]))
            prob = prob_of(d, like, h, part)
            dscore = (prob * (ready.pop(0) - delta[h, 0:1, cols_of(part)])).astype(BF16)
            low, high = key_range(like, part, block)
            weights[h, key_rows(d, low, high), cols_of(part)] = dscore
            if late is not None:
                products(*late)
            late = (h, part, prob.astype(BF16), dscore)
        products(*late)

    def block_grads(d, which):
        grads = part_sum[which] * (scale, 1.0)[which]
        return jnp.where(key_kept(d), grads, 0.0)

    forward_all(0, arrive_own, False, True)
    forward_all(2, arrive_two_back, False, True)
    forward_all(1, arrive_one_back, False)
    forward_all(3, arrive_three_back, True)

    def grads_back(which):
        return remote(
            sent.at[0, which], came.at[0, which], r_send.at[0, which], r_recv.at[0, which], cp_at(-1)
        )

    def grads_beside(which):
        return remote(
            sent.at[1, which],
            came.at[1, which],
            r_send.at[1, which],
            r_recv.at[1, which],
            cp_at(1 - 2 * core),
        )

    def grads_chip(which):
        return remote(
            sent.at[2, which], came.at[2, which], r_send.at[2, which], r_recv.at[2, which], cp_at(-2)
        )

    backward_all(3, 3)
    for which in (1, 0):
        sent[0, which] = block_grads(3, which).astype(BF16)
        grads_back(which).start()

    second = 1 + core
    backward_all(second, 1)
    for which in (1, 0):
        grads = block_grads(second, which)

        @pl.when(core == 0)
        def _(which=which, grads=grads):
            sent[1, which] = grads.astype(BF16)
            grads_beside(which).start()

        @pl.when(core == 1)
        def _(which=which, grads=grads):
            held[which] = grads

    third = 2 - core

    def third_done(which):
        grads = block_grads(third, which)

        @pl.when(core == 0)
        def _():
            grads_back(which).wait_recv()
            sent[2, which] = (grads + came[0, which].astype(F32)).astype(BF16)
            grads_chip(which).start()

        @pl.when(core == 1)
        def _():
            sent[1, which] = grads.astype(BF16)
            grads_beside(which).start()

    def third_halfway():
        @pl.when(core == 1)
        def _():
            for which in (1, 0):
                grads_back(which).wait_recv()
                grads_beside(which).wait_recv()
                others = came[0, which].astype(F32) + came[1, which].astype(F32)
                sent[2, which] = (held[which] + others).astype(BF16)
                grads_chip(which).start()

        third_done(1)

    backward_all(third, 2, third_halfway, True)
    third_done(0)

    def give(which, step):
        target = (dk_ref, dv_ref)[which]
        peer = lax.rem(hd + step, n_hd)
        return remote(
            final.at[which, pl.ds(pl.multiple_of(peer * rows, rows), rows)],
            target.at[:, columns(hd)],
            f_send.at[which, step],
            f_recv.at[which, step],
            {"hd": peer},
        )

    def give_own(which):
        target = (dk_ref, dv_ref)[which]
        return pltpu.make_async_copy(
            final.at[which, pl.ds(pl.multiple_of(hd * rows, rows), rows)],
            target.at[:, columns(hd)],
            local_sem.at[which],
        )

    def finish_own(which):
        grads_chip(which).wait_recv()
        whole = part_sum[which] * (scale, 1.0)[which] + came[2, which].astype(F32)

        @pl.when(core == 0)
        def _():
            grads_beside(which).wait_recv()
            final[which] = (whole + came[1, which].astype(F32)).astype(BF16)

        @pl.when(core == 1)
        def _():
            final[which] = whole.astype(BF16)

        for step in order:
            give(which, step).start()
        give_own(which).start()

    def grad_queries(some):
        for h in some:
            for part in range(2):
                reach = pl.ds(part * HALF, REACH * block + HALF)
                term = dot(kt[:, reach], weights[h, reach, cols_of(part)]) * scale
                dqb[h, cols_of(part), :] = term.astype(BF16).T
            store(1, h).start()

    backward_all(0, 0, lambda: finish_own(1), True)
    early = heads // 4
    grad_queries(range(early))
    finish_own(0)
    grad_queries(range(early, heads))

    for which in range(2):
        for step in order:
            give(which, step).wait_recv()
        give_own(which).wait()
    for which in range(2):
        for step in order:
            exchange(which, step).wait_send()
            give(which, step).wait_send()
        ahead(which).wait_send()
        beside_even(which).wait_send()
        onward(which).wait_send()
        grads_back(which).wait_send()
        grads_beside(which).wait_send()
        grads_chip(which).wait_send()
        for h in range(heads):
            store(which, h).wait()


def pieces(shape):
    step = min(shape[0], 128)
    return [slice(at, at + step) for at in range(0, shape[0], step)]


def hand_over(count, *refs):
    sources, targets, held = refs[:count], refs[count : 2 * count], refs[2 * count : 3 * count]
    in_sem, out_sem = refs[3 * count :]
    loads, stores = [], []
    for source, target, hold in zip(sources, targets, held):
        for at in pieces(source.shape):
            i = len(loads)
            loads.append(pltpu.make_async_copy(source.at[at], hold.at[at], in_sem.at[i]))
            stores.append(pltpu.make_async_copy(hold.at[at], target.at[at], out_sem.at[i]))
    for copy in loads:
        copy.start()
    for load, store in zip(loads, stores):
        load.wait()
        store.start()
    for copy in stores:
        copy.wait()


def on_device(n_cp, n_hd, queries, keys, values, grads_out, doc_lengths):
    block, width = queries.shape
    heads = width // HD
    blocks = REACH + 1
    vmem = pltpu.VMEM
    dma = pltpu.SemaphoreType.DMA
    anywhere = pl.BlockSpec(memory_space=pl.ANY)
    products = 6 * heads * 14 * HALF * HALF * HD * 2
    results = pl.pallas_call(
        functools.partial(kernel, n_cp, n_hd, heads, block),
        out_shape=(
            jax.ShapeDtypeStruct(queries.shape, BF16),
            jax.ShapeDtypeStruct(queries.shape, BF16),
            jax.ShapeDtypeStruct(keys.shape, BF16),
            jax.ShapeDtypeStruct(values.shape, BF16),
        ),
        in_specs=[pl.BlockSpec(memory_space=pltpu.SMEM)] + [anywhere] * 4,
        out_specs=(anywhere,) * 4,
        scratch_shapes=[
            vmem((heads, block, HD), BF16),
            vmem((heads, block, HD), BF16),
            vmem((heads, 2 * HD, block), BF16),
            vmem((heads, HD, block), BF16),
            vmem((blocks, 2, block, HD), BF16),
            vmem((blocks, block, HD), BF16),
            vmem((HD, blocks * block), BF16),
            vmem((blocks, HD + ONES, block), BF16),
            vmem((8, block), jnp.int32),
            vmem((ONES, block), jnp.int32),
            vmem((block, block), F32),
            vmem((heads, blocks * block, block), BF16),
            vmem((blocks, heads, HD, block), F32),
            vmem((blocks, heads, 8, block), F32),
            vmem((blocks, heads, 8, block), F32),
            vmem((heads, 8, block), F32),
            vmem((heads, block, HD), BF16),
            vmem((heads, block, HD), BF16),
            vmem((2, block, HD), F32),
            vmem((2, block, HD), F32),
            vmem((3, 2, block, HD), BF16),
            vmem((3, 2, block, HD), BF16),
            vmem((2, block, HD), BF16),
            dma((2, heads)),
            dma((2, heads)),
            dma((2,)),
            dma((2, n_hd)),
            dma((2, n_hd)),
            dma((3, 2)),
            dma((4, 2)),
            dma((3, 2)),
            dma((3, 2)),
            dma((2, n_hd)),
            dma((2, n_hd)),
        ],
        compiler_params=pltpu.CompilerParams(
            collective_id=0, has_side_effects=True, vmem_limit_bytes=56 * 2**20
        ),
        cost_estimate=pl.CostEstimate(
            flops=products, bytes_accessed=8 * 2**20, transcendentals=products // (12 * HD)
        ),
    )(doc_lengths, keys, values, queries, grads_out)

    count = sum(len(pieces(one.shape)) for one in results)
    return pl.pallas_call(
        functools.partial(hand_over, len(results)),
        out_shape=tuple(jax.ShapeDtypeStruct(one.shape, one.dtype) for one in results),
        in_specs=[anywhere] * len(results),
        out_specs=(anywhere,) * len(results),
        scratch_shapes=[vmem(one.shape, one.dtype) for one in results]
        + [dma((count,)), dma((count,))],
        compiler_params=pltpu.CompilerParams(vmem_limit_bytes=56 * 2**20),
    )(*results)


def solution(mesh):
    in_specs = (P("cp", "hd"), P(("cp", "hd"), None), P(("cp", "hd"), None), P("cp", "hd"), P())
    out_specs = (P("cp", "hd"), P("cp", "hd"), P(("cp", "hd"), None), P(("cp", "hd"), None))
    return jax.shard_map(
        functools.partial(on_device, mesh.shape["cp"], mesh.shape["hd"]),
        mesh=mesh,
        in_specs=in_specs,
        out_specs=out_specs,
        check_vma=False,
    )
```

```python
import functools
import math

import jax
import jax.numpy as jnp
from jax import lax
from jax.experimental import pallas as pl
from jax.experimental.pallas import tpu as pltpu
from jax.sharding import PartitionSpec as P

HD = 128
REACH = 3
HALF = 256
ONES = 16
MASKED = -1e30
FLOOR = -5e29
CEILING = 1e30
MESH = pl.DeviceIdType.MESH
F32 = jnp.float32
BF16 = jnp.bfloat16


def dot(a, b):
    return jnp.dot(a, b, preferred_element_type=F32)


def key_range(distance, part, block):
    if distance == 0 and part == 0:
        return 0, HALF
    if distance == REACH and part == 1:
        return HALF, block
    return 0, block


def kernel(
    n_cp,
    n_hd,
    heads,
    block,
    doc_ref,
    k_ref,
    v_ref,
    q_ref,
    g_ref,
    out_ref,
    dq_ref,
    dk_ref,
    dv_ref,
    qs,
    gs,
    qt,
    gt,
    kv,
    ks,
    kt,
    vt,
    first,
    begin,
    bias,
    weights,
    acc,
    top,
    total,
    delta,
    own_dprob,
    outt,
    outb,
    dqb,
    part_sum,
    held,
    sent,
    came,
    final,
    load_sem,
    store_sem,
    local_sem,
    a_send,
    a_recv,
    x_send,
    x_recv,
    r_send,
    r_recv,
    f_send,
    f_recv,
):
    cp = lax.axis_index("cp")
    hd = lax.axis_index("hd")
    core = lax.rem(cp, 2)
    rows = block // n_hd
    scale = 1.0 / math.sqrt(HD)
    log_scale = scale * math.log2(math.e)

    def cp_at(step):
        return {"cp": lax.rem(cp + step + n_cp, n_cp)}

    def hd_at(step):
        return {"hd": lax.rem(hd + step, n_hd)}

    def columns(index):
        return pl.ds(pl.multiple_of(index * HD, HD), HD)

    def remote(src, dst, send_sem, recv_sem, device):
        return pltpu.make_async_remote_copy(
            src_ref=src,
            dst_ref=dst,
            send_sem=send_sem,
            recv_sem=recv_sem,
            device_id=device,
            device_id_type=MESH,
        )

    def load(which, h):
        source, target = ((q_ref, qs), (g_ref, gs))[which]
        return pltpu.make_async_copy(
            source.at[:, columns(h)], target.at[h], load_sem.at[which, h]
        )

    def store(which, h):
        source, target = ((outb, out_ref), (dqb, dq_ref))[which]
        return pltpu.make_async_copy(
            source.at[h], target.at[:, columns(h)], store_sem.at[which, h]
        )

    barrier = pltpu.get_barrier_semaphore()
    for step in range(1, n_hd):
        pl.semaphore_signal(barrier, inc=1, device_id=hd_at(step), device_id_type=MESH)
    for step in (-2, -1, 1, 2):
        pl.semaphore_signal(barrier, inc=1, device_id=cp_at(step), device_id_type=MESH)
    for which in range(2):
        for h in range(heads):
            load(which, h).start()
    pl.semaphore_wait(barrier, n_hd - 1 + 4)

    def exchange(which, step):
        source = (k_ref, v_ref)[which]
        peer = lax.rem(hd + step, n_hd)
        return remote(
            source.at[:, columns(peer)],
            kv.at[0, which, pl.ds(pl.multiple_of(hd * rows, rows), rows)],
            a_send.at[which, step],
            a_recv.at[which, step],
            {"hd": peer},
        )

    def exchange_own(which):
        source = (k_ref, v_ref)[which]
        return pltpu.make_async_copy(
            source.at[:, columns(hd)],
            kv.at[0, which, pl.ds(pl.multiple_of(hd * rows, rows), rows)],
            local_sem.at[which],
        )

    order = sorted(range(1, n_hd), key=lambda step: -min(step, n_hd - step))
    for which in range(2):
        for step in order:
            exchange(which, step).start()
        exchange_own(which).start()

    def ahead(which, step=None):
        part = kv.at[0, which]
        target = kv.at[2, which]
        if step is not None:
            owner = lax.rem(hd - step + n_hd, n_hd)
            at = pl.ds(pl.multiple_of(owner * rows, rows), rows)
            part, target = part.at[at], target.at[at]
        return remote(part, target, x_send.at[0, which], x_recv.at[2, which], cp_at(2))

    def beside_even(which):
        return remote(
            kv.at[0, which], kv.at[1, which], x_send.at[1, which], x_recv.at[1, which], cp_at(1)
        )

    def beside_odd(which):
        return remote(
            kv.at[2, which], kv.at[1, which], x_send.at[1, which], x_recv.at[1, which], cp_at(-1)
        )

    def onward(which):
        return remote(
            kv.at[2, which], kv.at[3, which], x_send.at[2, which], x_recv.at[3, which], cp_at(1)
        )

    position = cp * block + lax.broadcasted_iota(jnp.int32, (8, block), 1)
    corner = jnp.full((ONES, block), cp * block, jnp.int32)

    def next_doc(i, carry):
        edge, start, start_first = carry
        edge = edge + doc_ref[i]
        return (
            edge,
            jnp.where(position >= edge, edge, start),
            jnp.where(corner >= edge, edge, start_first),
        )

    _, start, start_first = lax.fori_loop(
        0,
        doc_ref.shape[0],
        next_doc,
        (jnp.int32(0), jnp.zeros((8, block), jnp.int32), jnp.zeros((ONES, block), jnp.int32)),
    )
    first[...] = start - cp * block
    begin[...] = start_first - cp * block

    def mask_rows(i, _):
        rows_at = pl.ds(pl.multiple_of(i * 64, 64), 64)
        key_pos = lax.broadcasted_iota(jnp.int32, (64, block), 0) + i * 64
        query_pos = lax.broadcasted_iota(jnp.int32, (64, block), 1)
        allowed = (key_pos >= first[0:1, :]) & (key_pos <= query_pos)
        bias[rows_at, :] = jnp.where(allowed, 0.0, MASKED)
        return 0

    lax.fori_loop(0, block // 64, mask_rows, 0)

    for which in range(2):
        for h in range(heads):
            load(which, h).wait()

    def turn_queries(h, _):
        scaled = qs[h].astype(F32).T * log_scale
        high = scaled.astype(BF16)
        qt[h, :HD, :] = high
        qt[h, HD:, :] = (scaled - high.astype(F32)).astype(BF16)
        gt[h] = gs[h].T
        return 0

    lax.fori_loop(0, heads, turn_queries, 0)

    def arrive_own(which):
        exchange_own(which).wait()
        ahead(which, 0).start()
        for step in reversed(order):
            exchange(which, step).wait_recv()
            ahead(which, step).start()

        @pl.when(core == 0)
        def _():
            beside_even(which).start()

    def arrive_two_back(which):
        ahead(which).wait_recv()
        onward(which).start()

        @pl.when(core == 1)
        def _():
            beside_odd(which).start()

    def arrive_one_back(which):
        beside_even(which).wait_recv()

    def arrive_three_back(which):
        onward(which).wait_recv()

    def key_rows(d, low=0, high=block):
        begin_at = (REACH - d) * block + low
        if not isinstance(d, int):
            begin_at = pl.multiple_of(begin_at, HALF)
        return pl.ds(begin_at, high - low)

    def key_kept(d):
        key_pos = lax.broadcasted_iota(jnp.int32, (block, HD), 0) - d * block
        return key_pos >= begin[0:1, :HD]

    def turn_keys(d):
        keys = kv[d, 0]
        if d == 0:
            ks[d] = keys
            kt[:, key_rows(d)] = keys.T
        else:
            kept = key_kept(d)
            wide = keys.astype(F32)
            ks[d] = jnp.where(kept, wide, wide[block - 1 :, :]).astype(BF16)
            kt[:, key_rows(d)] = jnp.where(kept, wide, 0.0).astype(BF16).T

    def turn_values(d):
        values = kv[d, 1]
        if d == 0:
            vt[d, :HD, :] = values.T
            vt[d, HD:, :] = jnp.ones((ONES, block), BF16)
        else:
            vt[d, :HD, :] = jnp.where(key_kept(d), values.astype(F32), 0.0).astype(BF16).T
            key_pos = lax.broadcasted_iota(jnp.int32, (ONES, block), 1) - d * block
            vt[d, HD:, :] = jnp.where(key_pos >= begin[...], 1.0, 0.0).astype(BF16)

    items = [(h, part) for h in range(heads) for part in range(2)]

    def cols_of(part):
        return slice(part * HALF, (part + 1) * HALF)

    def forward_all(d, arrive, last, values_last=False):
        arrive(0)
        turn_keys(d)

        def scores_of(h, part):
            low, high = key_range(d, part, block)
            keys = ks[d, low:high, :]
            return dot(jnp.concatenate([keys, keys], axis=1), qt[h, :, cols_of(part)])

        def softmax(h, part, scores):
            cols = cols_of(part)
            low, high = key_range(d, part, block)
            if d == 0:
                scores = scores + bias[low:high, cols]
                peak = jnp.max(scores, axis=0, keepdims=True)
                kept_peak = peak
            else:
                reached = first[0:1, cols] < (1 - d) * block
                peak = jnp.max(scores, axis=0, keepdims=True)
                kept_peak = jnp.where(reached, peak, FLOOR)
                peak = jnp.where(reached, peak, CEILING)
            tile = jnp.exp2(scores - peak).astype(BF16)
            weights[h, key_rows(d, low, high), cols] = tile
            top[d, h, :, cols] = jnp.broadcast_to(kept_peak, (8, HALF))
            return tile

        def weighted(h, part, tile):
            cols = cols_of(part)
            low, high = key_range(d, part, block)
            value = dot(vt[d, :, low:high], tile)
            acc[d, h, :, cols] = value[:HD]
            total[d, h, :, cols] = value[HD : HD + 8]
            if last and part == 1:
                finish(h)

        ready = [scores_of(*item) for item in items[:2]]
        late = None
        for i, item in enumerate(items):
            if i + 2 < len(items):
                ready.append(scores_of(*items[i + 2]))
            tile = softmax(*item, ready.pop(0))
            if values_last:
                continue
            if late is None:
                arrive(1)
                turn_values(d)
            else:
                weighted(*late)
            late = (*item, tile)
        if values_last:
            arrive(1)
            turn_values(d)
            for h, part in items:
                low, high = key_range(d, part, block)
                weighted(h, part, weights[h, key_rows(d, low, high), cols_of(part)])
        else:
            weighted(*late)

    def finish(h):
        peaks = [top[d, h] for d in range(REACH + 1)]
        peak = functools.reduce(jnp.maximum, peaks)
        factors = [jnp.exp2(one - peak) for one in peaks]
        sums = functools.reduce(
            jnp.add, [factors[d] * total[d, h] for d in range(REACH + 1)]
        )
        inverse = 1.0 / sums
        value = None
        for d in range(REACH + 1):
            factor = factors[d] * inverse
            top[d, h] = factor
            term = acc[d, h] * factor[0:1]
            value = term if value is None else value + term
        rounded = value.astype(BF16)
        delta[h] = jnp.broadcast_to(
            jnp.sum(gt[h].astype(F32) * rounded.astype(F32), axis=0, keepdims=True), (8, block)
        )
        outt[h] = rounded

    def prob_of(d, like, h, part):
        cols = cols_of(part)
        low, high = key_range(like, part, block)
        return weights[h, key_rows(d, low, high), cols].astype(F32) * top[d, h, 0:1, cols]

    def add_values(d, like, h, part, prob):
        low, high = key_range(like, part, block)
        part_sum[1, low:high, :] += dot(prob, gs[h, cols_of(part), :])

    def backward_all(d, like, halfway=None, values_first=False):
        part_sum[...] = jnp.zeros_like(part_sum)
        if values_first:
            for h, part in items:
                add_values(d, like, h, part, prob_of(d, like, h, part).astype(BF16))

        def dprob_of(h, part):
            if like == 0:
                return None
            low, high = key_range(like, part, block)
            return dot(kv[d, 1, low:high, :], gt[h, :, cols_of(part)])

        def products(h, part, prob, dscore):
            low, high = key_range(like, part, block)
            part_sum[0, low:high, :] += dot(dscore, qs[h, cols_of(part), :])
            if not values_first:
                add_values(d, like, h, part, prob)

        ready = [dprob_of(*item) for item in items[:2]]
        late = None
        for i, (h, part) in enumerate(items):
            if halfway is not None and i == heads:
                halfway()
            if i + 2 < len(items):
                ready.append(dprob_of(*items[i + 2]))
            prob = prob_of(d, like, h, part)
            low, high = key_range(like, part, block)
            dprob = ready.pop(0)
            if dprob is None:
                dprob = own_dprob[h, low:high, cols_of(part)]
            dscore = (prob * (dprob - delta[h, 0:1, cols_of(part)])).astype(BF16)
            weights[h, key_rows(d, low, high), cols_of(part)] = dscore
            if late is not None:
                products(*late)
            late = (h, part, prob.astype(BF16), dscore)
        products(*late)

    def block_grads(d, which):
        grads = part_sum[which] * (scale, 1.0)[which]
        return jnp.where(key_kept(d), grads, 0.0)

    forward_all(0, arrive_own, False, True)
    for h, part in items:
        low, high = key_range(0, part, block)
        own_dprob[h, low:high, cols_of(part)] = dot(kv[0, 1, low:high, :], gt[h, :, cols_of(part)])
    forward_all(2, arrive_two_back, False, True)
    forward_all(1, arrive_one_back, False)
    forward_all(3, arrive_three_back, True)

    def grads_back(which):
        return remote(
            sent.at[0, which], came.at[0, which], r_send.at[0, which], r_recv.at[0, which], cp_at(-1)
        )

    def grads_beside(which):
        return remote(
            sent.at[1, which],
            came.at[1, which],
            r_send.at[1, which],
            r_recv.at[1, which],
            cp_at(1 - 2 * core),
        )

    def grads_chip(which):
        return remote(
            sent.at[2, which], came.at[2, which], r_send.at[2, which], r_recv.at[2, which], cp_at(-2)
        )

    backward_all(3, 3)
    for which in (1, 0):
        sent[0, which] = block_grads(3, which).astype(BF16)
        grads_back(which).start()

    second = 1 + core
    backward_all(second, 1)
    for which in (1, 0):
        grads = block_grads(second, which)

        @pl.when(core == 0)
        def _(which=which, grads=grads):
            sent[1, which] = grads.astype(BF16)
            grads_beside(which).start()

        @pl.when(core == 1)
        def _(which=which, grads=grads):
            held[which] = grads

    third = 2 - core

    def third_done(which):
        grads = block_grads(third, which)

        @pl.when(core == 0)
        def _():
            grads_back(which).wait_recv()
            sent[2, which] = (grads + came[0, which].astype(F32)).astype(BF16)
            grads_chip(which).start()

        @pl.when(core == 1)
        def _():
            sent[1, which] = grads.astype(BF16)
            grads_beside(which).start()

    def third_halfway():
        @pl.when(core == 1)
        def _():
            for which in (1, 0):
                grads_back(which).wait_recv()
                grads_beside(which).wait_recv()
                others = came[0, which].astype(F32) + came[1, which].astype(F32)
                sent[2, which] = (held[which] + others).astype(BF16)
                grads_chip(which).start()

        third_done(1)

    backward_all(third, 2, third_halfway, True)
    third_done(0)

    def give(which, step):
        target = (dk_ref, dv_ref)[which]
        peer = lax.rem(hd + step, n_hd)
        return remote(
            final.at[which, pl.ds(pl.multiple_of(peer * rows, rows), rows)],
            target.at[:, columns(hd)],
            f_send.at[which, step],
            f_recv.at[which, step],
            {"hd": peer},
        )

    def give_own(which):
        target = (dk_ref, dv_ref)[which]
        return pltpu.make_async_copy(
            final.at[which, pl.ds(pl.multiple_of(hd * rows, rows), rows)],
            target.at[:, columns(hd)],
            local_sem.at[which],
        )

    def finish_own(which):
        grads_chip(which).wait_recv()
        whole = part_sum[which] * (scale, 1.0)[which] + came[2, which].astype(F32)

        @pl.when(core == 0)
        def _():
            grads_beside(which).wait_recv()
            final[which] = (whole + came[1, which].astype(F32)).astype(BF16)

        @pl.when(core == 1)
        def _():
            final[which] = whole.astype(BF16)

        for step in order:
            give(which, step).start()
        give_own(which).start()

    def grad_queries():
        for h in range(heads):
            outb[h] = outt[h].T
            store(0, h).start()
            for part in range(2):
                reach = pl.ds(part * HALF, REACH * block + HALF)
                term = dot(kt[:, reach], weights[h, reach, cols_of(part)]) * scale
                dqb[h, cols_of(part), :] = term.astype(BF16).T
            store(1, h).start()

    backward_all(0, 0, lambda: finish_own(1), True)
    finish_own(0)
    grad_queries()

    for which in range(2):
        for step in order:
            give(which, step).wait_recv()
        give_own(which).wait()
    for which in range(2):
        for step in order:
            exchange(which, step).wait_send()
            give(which, step).wait_send()
        ahead(which).wait_send()
        beside_even(which).wait_send()
        onward(which).wait_send()
        grads_back(which).wait_send()
        grads_beside(which).wait_send()
        grads_chip(which).wait_send()
        for h in range(heads):
            store(which, h).wait()


def pieces(shape):
    step = min(shape[0], 128)
    return [slice(at, at + step) for at in range(0, shape[0], step)]


def hand_over(count, *refs):
    sources, targets, held = refs[:count], refs[count : 2 * count], refs[2 * count : 3 * count]
    in_sem, out_sem = refs[3 * count :]
    loads, stores = [], []
    for source, target, hold in zip(sources, targets, held):
        for at in pieces(source.shape):
            i = len(loads)
            loads.append(pltpu.make_async_copy(source.at[at], hold.at[at], in_sem.at[i]))
            stores.append(pltpu.make_async_copy(hold.at[at], target.at[at], out_sem.at[i]))
    for copy in loads:
        copy.start()
    for load, store in zip(loads, stores):
        load.wait()
        store.start()
    for copy in stores:
        copy.wait()


def on_device(n_cp, n_hd, queries, keys, values, grads_out, doc_lengths):
    block, width = queries.shape
    heads = width // HD
    blocks = REACH + 1
    vmem = pltpu.VMEM
    dma = pltpu.SemaphoreType.DMA
    anywhere = pl.BlockSpec(memory_space=pl.ANY)
    products = 6 * heads * 14 * HALF * HALF * HD * 2
    results = pl.pallas_call(
        functools.partial(kernel, n_cp, n_hd, heads, block),
        out_shape=(
            jax.ShapeDtypeStruct(queries.shape, BF16),
            jax.ShapeDtypeStruct(queries.shape, BF16),
            jax.ShapeDtypeStruct(keys.shape, BF16),
            jax.ShapeDtypeStruct(values.shape, BF16),
        ),
        in_specs=[pl.BlockSpec(memory_space=pltpu.SMEM)] + [anywhere] * 4,
        out_specs=(anywhere,) * 4,
        scratch_shapes=[
            vmem((heads, block, HD), BF16),
            vmem((heads, block, HD), BF16),
            vmem((heads, 2 * HD, block), BF16),
            vmem((heads, HD, block), BF16),
            vmem((blocks, 2, block, HD), BF16),
            vmem((blocks, block, HD), BF16),
            vmem((HD, blocks * block), BF16),
            vmem((blocks, HD + ONES, block), BF16),
            vmem((8, block), jnp.int32),
            vmem((ONES, block), jnp.int32),
            vmem((block, block), F32),
            vmem((heads, blocks * block, block), BF16),
            vmem((blocks, heads, HD, block), F32),
            vmem((blocks, heads, 8, block), F32),
            vmem((blocks, heads, 8, block), F32),
            vmem((heads, 8, block), F32),
            vmem((heads, block, block), F32),
            vmem((heads, HD, block), BF16),
            vmem((heads, block, HD), BF16),
            vmem((heads, block, HD), BF16),
            vmem((2, block, HD), F32),
            vmem((2, block, HD), F32),
            vmem((3, 2, block, HD), BF16),
            vmem((3, 2, block, HD), BF16),
            vmem((2, block, HD), BF16),
            dma((2, heads)),
            dma((2, heads)),
            dma((2,)),
            dma((2, n_hd)),
            dma((2, n_hd)),
            dma((3, 2)),
            dma((4, 2)),
            dma((3, 2)),
            dma((3, 2)),
            dma((2, n_hd)),
            dma((2, n_hd)),
        ],
        compiler_params=pltpu.CompilerParams(
            collective_id=0, has_side_effects=True, vmem_limit_bytes=56 * 2**20
        ),
        cost_estimate=pl.CostEstimate(
            flops=products, bytes_accessed=8 * 2**20, transcendentals=products // (12 * HD)
        ),
    )(doc_lengths, keys, values, queries, grads_out)

    count = sum(len(pieces(one.shape)) for one in results)
    return pl.pallas_call(
        functools.partial(hand_over, len(results)),
        out_shape=tuple(jax.ShapeDtypeStruct(one.shape, one.dtype) for one in results),
        in_specs=[anywhere] * len(results),
        out_specs=(anywhere,) * len(results),
        scratch_shapes=[vmem(one.shape, one.dtype) for one in results]
        + [dma((count,)), dma((count,))],
        compiler_params=pltpu.CompilerParams(vmem_limit_bytes=56 * 2**20),
    )(*results)


def solution(mesh):
    in_specs = (P("cp", "hd"), P(("cp", "hd"), None), P(("cp", "hd"), None), P("cp", "hd"), P())
    out_specs = (P("cp", "hd"), P("cp", "hd"), P(("cp", "hd"), None), P(("cp", "hd"), None))
    return jax.shard_map(
        functools.partial(on_device, mesh.shape["cp"], mesh.shape["hd"]),
        mesh=mesh,
        in_specs=in_specs,
        out_specs=out_specs,
        check_vma=False,
    )
```
